32 devices in a mesh: team: 16 (over z, x, core), member: 2 (over y).
Axes of the slice: x: 2, y: 2, z: 4, core: 2. Of those that a mesh axis runs over, the one named last changes fastest.
Arguments:
- embeddings: float32 [16384, 256], P('team'), may hold values from -1 to 1, as said below
Outputs:
- forces: float32 [16384, 256], P(('team', 'member'))
The draws below stay inside these ranges and needn't reach their ends.
Inputs may be any that keep to these rules, and one draw needn't show every extreme that they name: `embeddings`: every row has Euclidean length one.
All inputs are finite; a program needn't handle non-finite values.
Results may differ from the reference program's by a relative error of at most 0.00005.
Values sent between devices are 32-bit elements; how exact they have to be, the bound alone decides.
No kernel may reach another device: no remote copies, remote signals or barrier semaphores. Data moves between devices by JAX's collectives and lax.ppermute only.
A program may use at most 64 MiB of HBM per device.

```python
import math
import jax
import jax.numpy as jnp
from jax import lax

D = 256
ROWS = 1024
TOTAL = 16384


def unit_rows(values):
    return values / jnp.sqrt(jnp.sum(values * values, axis=-1, keepdims=True))


def draw_embeddings(key, part):
    groups = max(TOTAL // 128, 2)
    k_centre = jax.random.fold_in(key, 11)
    k_assign = jax.random.fold_in(key, 12)
    k_noise = jax.random.fold_in(key, 13)
    k_spread = jax.random.fold_in(key, 14)
    centres = unit_rows(jax.random.normal(k_centre, (groups, D), jnp.float32))
    assigned = jax.random.randint(k_assign, (TOTAL,), 0, groups)
    spread_level = jnp.exp(jax.random.uniform(k_spread, (groups,), jnp.float32, math.log(0.3), math.log(0.8)))
    noise_part = jax.random.normal(k_noise, (TOTAL, D), jnp.float32)
    raw_rows = centres[assigned] + spread_level[assigned][:, None] * noise_part / math.sqrt(D)
    return unit_rows(raw_rows)


def setup_inputs(seed: int = 0) -> dict:
    arg_keys = jax.random.split(jax.random.key(seed), 2)
    return {
        "embeddings": draw_embeddings(jax.random.fold_in(arg_keys[1], 71), 0),
    }


def reference(embeddings):
    blocks = embeddings.reshape(-1, ROWS, D)

    def one_block(rows):
        similarity = jnp.dot(rows, embeddings.T, precision=lax.Precision.HIGHEST, preferred_element_type=jnp.float32)
        weights = jnp.exp(2.0 * similarity - 2.0)
        return jnp.dot(weights, embeddings, precision=lax.Precision.HIGHEST, preferred_element_type=jnp.float32)

    return lax.map(one_block, blocks).reshape(TOTAL, D)
```

```python
import jax
import jax.numpy as jnp
from jax import lax
from jax.sharding import PartitionSpec as P

CORES = 2
COLUMNS = 2


def moved(value, axis, target):
    count = lax.axis_size(axis)
    pairs = [(source, target(source)) for source in range(count)]
    return lax.ppermute(value, axis, [pair for pair in pairs if pair[1] is not None])


def core_swap(value):
    return moved(value, "team", lambda team: team ^ 1)


def column_swap(value):
    return moved(value, "team", lambda team: team ^ CORES)


def along_line(value, target):
    line = CORES * COLUMNS

    def team_target(team):
        layer = target(team // line)
        return None if layer is None else layer * line + team % line

    return moved(value, "team", team_target)


def line_parts(part):
    layers = lax.axis_size("team") // (CORES * COLUMNS)
    if layers != 4:
        parts = []
        for _ in range(layers - 1):
            part = along_line(part, lambda layer: (layer + layers - 1) % layers)
            parts.append(part)
        return parts
    middle = {1: 2, 2: 1}.get
    outward = {1: 0, 2: 3}.get
    layer_index = lax.axis_index("team") // (CORES * COLUMNS)
    inner = (layer_index == 1) | (layer_index == 2)
    near = along_line(part, lambda layer: layer ^ 1)
    across = along_line(part, middle)
    across_far = along_line(near, middle)
    second = jnp.where(inner, across, along_line(across, outward))
    third = jnp.where(inner, across_far, along_line(across_far, outward))
    return [near, second, third]


def over_members(part):
    members = lax.axis_size("member")
    return [
        moved(part, "member", lambda member, step=step: (member + step) % members)
        for step in range(1, members)
    ]


def sums(rows, partners):
    similarity = lax.dot_general(
        rows,
        partners,
        (((1,), (1,)), ((), ())),
        precision=lax.Precision.HIGH,
        preferred_element_type=jnp.float32,
    )
    weights = jnp.exp(2.0 * similarity - 2.0)
    return jnp.dot(weights, partners, precision=lax.Precision.HIGH, preferred_element_type=jnp.float32)


def local(embeddings):
    members = lax.axis_size("member")
    share = embeddings.shape[0] // members
    part = lax.dynamic_slice_in_dim(embeddings, lax.axis_index("member") * share, share)
    partners = [embeddings]
    for piece in line_parts(part):
        partners.append(piece)
        partners.extend(over_members(piece))
    beside = column_swap(part)
    own_rows = jnp.concatenate([part, core_swap(part)])
    beside_rows = jnp.concatenate([beside, core_swap(beside)])
    own_sums = sum(sums(own_rows, piece) for piece in partners)
    beside_sums = sum(sums(beside_rows, piece) for piece in partners)
    returned = column_swap(beside_sums[:share] + core_swap(beside_sums[share:]))
    return own_sums[:share] + core_swap(own_sums[share:]) + returned


def solution(mesh):
    return jax.shard_map(
        local,
        mesh=mesh,
        in_specs=(P("team", None),),
        out_specs=P(("team", "member"), None),
        check_vma=False,
    )
```

```python
import jax
import jax.numpy as jnp
from jax import lax
from jax.sharding import PartitionSpec as P

CORES = 2
COLUMNS = 2


def moved(value, axis, target):
    count = lax.axis_size(axis)
    pairs = [(source, target(source)) for source in range(count)]
    return lax.ppermute(value, axis, [pair for pair in pairs if pair[1] is not None])


def core_swap(value):
    return moved(value, "team", lambda team: team ^ 1)


def column_swap(value):
    return moved(value, "team", lambda team: team ^ CORES)


def along_line(value, target):
    line = CORES * COLUMNS

    def team_target(team):
        layer = target(team // line)
        return None if layer is None else layer * line + team % line

    return moved(value, "team", team_target)


def over_members(part):
    members = lax.axis_size("member")
    return [
        moved(part, "member", lambda member, step=step: (member + step) % members)
        for step in range(1, members)
    ]


def sums(rows, partners):
    similarity = lax.dot_general(
        rows,
        partners,
        (((1,), (1,)), ((), ())),
        precision=lax.Precision.HIGH,
        preferred_element_type=jnp.float32,
    )
    weights = jnp.exp(2.0 * similarity - 2.0)
    return jnp.dot(weights, partners, precision=lax.Precision.HIGH, preferred_element_type=jnp.float32)


def plain(embeddings):
    members = lax.axis_size("member")
    layers = lax.axis_size("team") // (CORES * COLUMNS)
    share = embeddings.shape[0] // members
    part = lax.dynamic_slice_in_dim(embeddings, lax.axis_index("member") * share, share)
    partners = [embeddings]
    piece = part
    for _ in range(layers - 1):
        piece = along_line(piece, lambda layer: (layer + layers - 1) % layers)
        partners.append(piece)
        partners.extend(over_members(piece))
    beside = column_swap(part)
    own_rows = jnp.concatenate([part, core_swap(part)])
    beside_rows = jnp.concatenate([beside, core_swap(beside)])
    own_sums = sum(sums(own_rows, piece) for piece in partners)
    beside_sums = sum(sums(beside_rows, piece) for piece in partners)
    returned = column_swap(beside_sums[:share] + core_swap(beside_sums[share:]))
    return own_sums[:share] + core_swap(own_sums[share:]) + returned


def staged(embeddings):
    share = embeddings.shape[0] // 2
    stage = lax.optimization_barrier
    middle = {1: 2, 2: 1}.get
    outward = {1: 0, 2: 3}.get
    layer_index = lax.axis_index("team") // (CORES * COLUMNS)
    inner = (layer_index == 1) | (layer_index == 2)
    part = lax.dynamic_slice_in_dim(embeddings, lax.axis_index("member") * share, share)

    near = along_line(part, lambda layer: layer ^ 1)
    across = along_line(part, middle)
    beside = column_swap(part)
    own = [part, core_swap(part)]
    own_sums = [sums(rows, embeddings) for rows in own]

    near, across, own_sums = stage((near, across, own_sums))
    outer_second = along_line(across, outward)
    across_far = along_line(near, middle)
    (near_over,) = over_members(near)
    far = [beside, core_swap(beside)]
    far_sums = [sums(rows, embeddings) for rows in far]

    across, outer_second, across_far, own_sums, far_sums, near_over = stage(
        (across, outer_second, across_far, own_sums, far_sums, near_over)
    )
    outer_third = along_line(across_far, outward)
    second = jnp.where(inner, across, outer_second)
    (second_over,) = over_members(second)
    far_sums = add_sums(far_sums, far, near)
    far_sums = add_sums(far_sums, far, near_over)

    across_far, outer_third, own_sums, far_sums, second_over = stage(
        (across_far, outer_third, own_sums, far_sums, second_over)
    )
    third = jnp.where(inner, across_far, outer_third)
    (third_over,) = over_members(third)
    far_sums = add_sums(far_sums, far, second)
    far_sums = add_sums(far_sums, far, second_over)
    far_sums = add_sums(far_sums, far, third)

    third_over, own_sums, far_sums = stage((third_over, own_sums, far_sums))
    far_sums = add_sums(far_sums, far, third_over)

    summed = far_sums[0] + core_swap(far_sums[1])
    summed, third_over, own_sums = stage((summed, third_over, own_sums))
    returned = column_swap(summed)
    own_sums = add_sums(own_sums, own, near)
    own_sums = add_sums(own_sums, own, near_over)
    own_sums = add_sums(own_sums, own, second)
    own_sums = add_sums(own_sums, own, second_over)
    own_sums = add_sums(own_sums, own, third)
    own_sums = add_sums(own_sums, own, third_over)

    return own_sums[0] + core_swap(own_sums[1]) + returned


def add_sums(totals, rows, partners):
    return [total + sums(part, partners) for total, part in zip(totals, rows)]


def local(embeddings):
    layers = lax.axis_size("team") // (CORES * COLUMNS)
    return (staged if layers == 4 and lax.axis_size("member") == 2 else plain)(embeddings)


def solution(mesh):
    return jax.shard_map(
        local,
        mesh=mesh,
        in_specs=(P("team", None),),
        out_specs=P(("team", "member"), None),
        check_vma=False,
    )
```

```python
import functools
import math

import jax
import jax.numpy as jnp
from jax import lax
from jax.experimental import pallas as pl
from jax.experimental.pallas import tpu as pltpu
from jax.sharding import PartitionSpec as P

CORES = 2
COLUMNS = 2


def moved(value, axis, target):
    count = lax.axis_size(axis)
    pairs = [(source, target(source)) for source in range(count)]
    return lax.ppermute(value, axis, [pair for pair in pairs if pair[1] is not None])


def core_swap(value):
    return moved(value, "team", lambda team: team ^ 1)


def column_swap(value):
    return moved(value, "team", lambda team: team ^ CORES)


def along_line(value, target):
    line = CORES * COLUMNS

    def team_target(team):
        layer = target(team // line)
        return None if layer is None else layer * line + team % line

    return moved(value, "team", team_target)


def over_members(part):
    members = lax.axis_size("member")
    return [
        moved(part, "member", lambda member, step=step: (member + step) % members)
        for step in range(1, members)
    ]


def sums(rows, partners):
    similarity = lax.dot_general(
        rows,
        partners,
        (((1,), (1,)), ((), ())),
        precision=lax.Precision.HIGH,
        preferred_element_type=jnp.float32,
    )
    weights = jnp.exp(2.0 * similarity - 2.0)
    return jnp.dot(weights, partners, precision=lax.Precision.HIGH, preferred_element_type=jnp.float32)


def plain(embeddings):
    members = lax.axis_size("member")
    layers = lax.axis_size("team") // (CORES * COLUMNS)
    share = embeddings.shape[0] // members
    part = lax.dynamic_slice_in_dim(embeddings, lax.axis_index("member") * share, share)
    partners = [embeddings]
    piece = part
    for _ in range(layers - 1):
        piece = along_line(piece, lambda layer: (layer + layers - 1) % layers)
        partners.append(piece)
        partners.extend(over_members(piece))
    beside = column_swap(part)
    own_rows = jnp.concatenate([part, core_swap(part)])
    beside_rows = jnp.concatenate([beside, core_swap(beside)])
    own_sums = sum(sums(own_rows, piece) for piece in partners)
    beside_sums = sum(sums(beside_rows, piece) for piece in partners)
    returned = column_swap(beside_sums[:share] + core_swap(beside_sums[share:]))
    return own_sums[:share] + core_swap(own_sums[share:]) + returned


ROW_TILE = 256
PARTNER_TILE = 1024
VMEM_ONLY = pl.BlockSpec(memory_space=pltpu.VMEM)
NO_COST = pl.CostEstimate(flops=1, bytes_accessed=1, transcendentals=0)


def split_terms(values):
    high = values.astype(jnp.bfloat16)
    return high, (values - high.astype(jnp.float32)).astype(jnp.bfloat16)


def sums_kernel(*refs, jobs, n_pieces):
    def take(count):
        nonlocal refs
        taken, refs = refs[:count], refs[count:]
        return taken

    pieces = take(n_pieces)
    rows = [take(n_rows) for n_rows, _, _, _ in jobs]
    totals = [take(n_rows if given else 0) for n_rows, given, _, _ in jobs]
    outs = [take(n_rows) for n_rows, _, _, _ in jobs]
    terms = [[take(2) for _ in range(n_rows)] for n_rows, _, _, _ in jobs]
    partner_high, partner_low = refs
    place = 0
    for piece in pieces:
        span = slice(place, place + piece.shape[0])
        partner_high[span, :], partner_low[span, :] = split_terms(piece[...])
        place += piece.shape[0]
    for sources, targets in zip(rows, terms):
        for source, (high, low) in zip(sources, targets):
            high[...], low[...] = split_terms(source[...] * (2.0 / math.log(2.0)))
    for job, (n_rows, given, start, length) in enumerate(jobs):
        for first in range(0, length, PARTNER_TILE):
            span = slice(start + first, start + min(first + PARTNER_TILE, length))
            high, low = partner_high[span, :], partner_low[span, :]
            keys = jnp.concatenate([high, low, high], axis=1)
            values = jnp.concatenate([high, high, low], axis=0)
            for number in range(n_rows):
                row_high, row_low = terms[job][number]
                out = outs[job][number]
                for row in range(0, out.shape[0], ROW_TILE):
                    tile = slice(row, row + ROW_TILE)
                    similarity = lax.dot_general(
                        jnp.concatenate([row_high[tile, :], row_high[tile, :], row_low[tile, :]], axis=1),
                        keys,
                        (((1,), (1,)), ((), ())),
                        preferred_element_type=jnp.float32,
                    )
                    weight_high, weight_low = split_terms(jnp.exp2(similarity))
                    added = jnp.dot(
                        jnp.concatenate([weight_high, weight_low, weight_high], axis=1),
                        values,
                        preferred_element_type=jnp.float32,
                    )
                    if first:
                        added = out[tile, :] + added
                    elif given:
                        added = totals[job][number][tile, :] + added
                    out[tile, :] = added


def add_sums(pieces, *jobs):
    lengths = [piece.shape[0] for piece in pieces]
    width = pieces[0].shape[1]
    plan = tuple(
        (len(rows), totals is not None, sum(lengths[:first]), sum(lengths[first:last]))
        for totals, rows, first, last in jobs
    )
    rows = [part for job in jobs for part in job[1]]
    operands = [*pieces, *rows, *[part for job in jobs for part in job[0] or ()]]
    scratch = [pltpu.VMEM(part.shape, jnp.bfloat16) for part in rows for _ in range(2)]
    scratch += [pltpu.VMEM((sum(lengths), width), jnp.bfloat16)] * 2
    outs = pl.pallas_call(
        functools.partial(sums_kernel, jobs=plan, n_pieces=len(pieces)),
        out_shape=[jax.ShapeDtypeStruct(part.shape, jnp.float32) for part in rows],
        in_specs=[VMEM_ONLY] * len(operands),
        out_specs=[VMEM_ONLY] * len(rows),
        scratch_shapes=scratch,
        compiler_params=pltpu.CompilerParams(vmem_limit_bytes=32 << 20),
        cost_estimate=NO_COST,
    )(*operands)
    grouped = []
    for _, part_rows, _, _ in jobs:
        grouped.append(list(outs[: len(part_rows)]))
        outs = outs[len(part_rows) :]
    return grouped


def core_swap_parts(value):
    return jnp.concatenate([core_swap(rows) for rows in jnp.split(value, 2)])


def half(block, index):
    share = block.shape[0] // 2
    return lax.dynamic_slice_in_dim(block, index * share, share)


def staged(embeddings):
    share = embeddings.shape[0] // 2
    stage = lax.optimization_barrier
    member = lax.axis_index("member")
    layer_index = lax.axis_index("team") // (CORES * COLUMNS)
    inner = (layer_index == 1) | (layer_index == 2)

    part = half(embeddings, member)
    near = along_line(part, lambda layer: layer ^ 1)
    second = along_line(part, lambda layer: 3 - layer)
    block_swapped = core_swap(embeddings)
    beside = column_swap(part)
    own = [part, half(block_swapped, member)]
    other = [half(embeddings, 1 - member), half(block_swapped, 1 - member)]
    (own_sums,) = add_sums([embeddings], (None, own, 0, 1))
    own_sums, beside = stage((own_sums, beside))
    far = [beside, core_swap_parts(beside)]
    (far_sums,) = add_sums([embeddings], (None, far, 0, 1))

    far_sums, second, near = stage((far_sums, second, near))
    third = along_line(jnp.where(inner, second, part), {0: 2, 1: 0, 2: 3, 3: 1}.get)
    near_beside = column_swap(near)
    (second_over,) = over_members(second)
    other_sums, far_sums, own_sums = add_sums(
        [near, second], (None, other, 0, 1), (far_sums, far, 1, 2), (own_sums, own, 0, 2)
    )

    own_sums, far_sums, other_sums, third = stage((own_sums, far_sums, other_sums, third))
    first_half, second_half = third[: share // 2], third[share // 2 :]
    (third_over,) = over_members(first_half)
    third_beside = column_swap(second_half)
    other_sums, far_sums = add_sums(
        [near_beside, second_half, first_half, second_over], (other_sums, other, 0, 2), (far_sums, far, 2, 4)
    )

    third_over, third_beside, own_sums, far_sums, other_sums = stage(
        (third_over, third_beside, own_sums, far_sums, other_sums)
    )
    far_sums, other_sums = add_sums(
        [third_over, third_beside], (far_sums, far, 0, 1), (other_sums, other, 1, 2)
    )
    far_total = far_sums[0] + core_swap(far_sums[1])
    other_total = other_sums[0] + core_swap(other_sums[1])

    far_total, other_total, own_sums = stage((far_total, other_total, own_sums))
    far_returned = column_swap(far_total)
    (other_returned,) = over_members(other_total)
    (own_sums,) = add_sums([near_beside, second_over, third, third_over, third_beside], (own_sums, own, 0, 5))
    swapped = core_swap_parts(own_sums[1])
    return (own_sums[0] + swapped + far_returned + other_returned) * math.exp(-2.0)


def local(embeddings):
    layers = lax.axis_size("team") // (CORES * COLUMNS)
    return (staged if layers == 4 and lax.axis_size("member") == 2 else plain)(embeddings)


def solution(mesh):
    return jax.shard_map(
        local,
        mesh=mesh,
        in_specs=(P("team", None),),
        out_specs=P(("team", "member"), None),
        check_vma=False,
    )
```

```python
import functools
import math

import jax
import jax.numpy as jnp
from jax import lax
from jax.experimental import pallas as pl
from jax.experimental.pallas import tpu as pltpu
from jax.sharding import PartitionSpec as P

CORES = 2
COLUMNS = 2


def moved(value, axis, target):
    count = lax.axis_size(axis)
    pairs = [(source, target(source)) for source in range(count)]
    return lax.ppermute(value, axis, [pair for pair in pairs if pair[1] is not None])


def core_swap(value):
    return moved(value, "team", lambda team: team ^ 1)


def column_swap(value):
    return moved(value, "team", lambda team: team ^ CORES)


def along_line(value, target):
    line = CORES * COLUMNS

    def team_target(team):
        layer = target(team // line)
        return None if layer is None else layer * line + team % line

    return moved(value, "team", team_target)


def over_members(part):
    members = lax.axis_size("member")
    return [
        moved(part, "member", lambda member, step=step: (member + step) % members)
        for step in range(1, members)
    ]


def sums(rows, partners):
    similarity = lax.dot_general(
        rows,
        partners,
        (((1,), (1,)), ((), ())),
        precision=lax.Precision.HIGH,
        preferred_element_type=jnp.float32,
    )
    weights = jnp.exp(2.0 * similarity - 2.0)
    return jnp.dot(weights, partners, precision=lax.Precision.HIGH, preferred_element_type=jnp.float32)


def plain(embeddings):
    members = lax.axis_size("member")
    layers = lax.axis_size("team") // (CORES * COLUMNS)
    share = embeddings.shape[0] // members
    part = lax.dynamic_slice_in_dim(embeddings, lax.axis_index("member") * share, share)
    partners = [embeddings]
    piece = part
    for _ in range(layers - 1):
        piece = along_line(piece, lambda layer: (layer + layers - 1) % layers)
        partners.append(piece)
        partners.extend(over_members(piece))
    beside = column_swap(part)
    own_rows = jnp.concatenate([part, core_swap(part)])
    beside_rows = jnp.concatenate([beside, core_swap(beside)])
    own_sums = sum(sums(own_rows, piece) for piece in partners)
    beside_sums = sum(sums(beside_rows, piece) for piece in partners)
    returned = column_swap(beside_sums[:share] + core_swap(beside_sums[share:]))
    return own_sums[:share] + core_swap(own_sums[share:]) + returned


ROW_TILE = 256
PARTNER_TILE = 512
VMEM_ONLY = pl.BlockSpec(memory_space=pltpu.VMEM)
NO_COST = pl.CostEstimate(flops=1, bytes_accessed=1, transcendentals=0)


def split_terms(values):
    high = values.astype(jnp.bfloat16)
    return high, (values - high.astype(jnp.float32)).astype(jnp.bfloat16)


def sums_kernel(*refs, jobs, n_pieces):
    def take(count):
        nonlocal refs
        taken, refs = refs[:count], refs[count:]
        return taken

    pieces = take(n_pieces)
    rows = [take(n_rows) for n_rows, _, _, _ in jobs]
    totals = [take(n_rows if given else 0) for n_rows, given, _, _ in jobs]
    outs = [take(n_rows) for n_rows, _, _, _ in jobs]
    terms = [[take(2) for _ in range(n_rows)] for n_rows, _, _, _ in jobs]
    partner_high, partner_low = refs
    place = 0
    for piece in pieces:
        span = slice(place, place + piece.shape[0])
        partner_high[span, :], partner_low[span, :] = split_terms(piece[...])
        place += piece.shape[0]
    for sources, targets in zip(rows, terms):
        for source, (high, low) in zip(sources, targets):
            high[...], low[...] = split_terms(source[...] * (2.0 / math.log(2.0)))
    for job, (n_rows, given, start, length) in enumerate(jobs):
        for first in range(0, length, PARTNER_TILE):
            span = slice(start + first, start + min(first + PARTNER_TILE, length))
            high, low = partner_high[span, :], partner_low[span, :]
            keys = jnp.concatenate([high, low, high], axis=1)
            values = jnp.concatenate([high, high, low], axis=0)
            for number in range(n_rows):
                row_high, row_low = terms[job][number]
                out = outs[job][number]
                for row in range(0, out.shape[0], ROW_TILE):
                    tile = slice(row, row + ROW_TILE)
                    similarity = lax.dot_general(
                        jnp.concatenate([row_high[tile, :], row_high[tile, :], row_low[tile, :]], axis=1),
                        keys,
                        (((1,), (1,)), ((), ())),
                        preferred_element_type=jnp.float32,
                    )
                    weight_high, weight_low = split_terms(jnp.exp2(similarity))
                    added = jnp.dot(
                        jnp.concatenate([weight_high, weight_low, weight_high], axis=1),
                        values,
                        preferred_element_type=jnp.float32,
                    )
                    if first:
                        added = out[tile, :] + added
                    elif given:
                        added = totals[job][number][tile, :] + added
                    out[tile, :] = added


def add_sums(pieces, *jobs):
    lengths = [piece.shape[0] for piece in pieces]
    width = pieces[0].shape[1]
    plan = tuple(
        (len(rows), totals is not None, sum(lengths[:first]), sum(lengths[first:last]))
        for totals, rows, first, last in jobs
    )
    rows = [part for job in jobs for part in job[1]]
    operands = [*pieces, *rows, *[part for job in jobs for part in job[0] or ()]]
    scratch = [pltpu.VMEM(part.shape, jnp.bfloat16) for part in rows for _ in range(2)]
    scratch += [pltpu.VMEM((sum(lengths), width), jnp.bfloat16)] * 2
    outs = pl.pallas_call(
        functools.partial(sums_kernel, jobs=plan, n_pieces=len(pieces)),
        out_shape=[jax.ShapeDtypeStruct(part.shape, jnp.float32) for part in rows],
        in_specs=[VMEM_ONLY] * len(operands),
        out_specs=[VMEM_ONLY] * len(rows),
        scratch_shapes=scratch,
        compiler_params=pltpu.CompilerParams(vmem_limit_bytes=32 << 20),
        cost_estimate=NO_COST,
    )(*operands)
    grouped = []
    for _, part_rows, _, _ in jobs:
        grouped.append(list(outs[: len(part_rows)]))
        outs = outs[len(part_rows) :]
    return grouped


def half(block, index):
    share = block.shape[0] // 2
    return lax.dynamic_slice_in_dim(block, index * share, share)


def core_swap_parts(value, parts):
    return jnp.concatenate([core_swap(rows) for rows in jnp.split(value, parts)])


def staged(embeddings):
    share = embeddings.shape[0] // 2
    stage = lax.optimization_barrier
    member = lax.axis_index("member")
    layer_index = lax.axis_index("team") // (CORES * COLUMNS)
    inner = (layer_index == 1) | (layer_index == 2)

    part = half(embeddings, member)
    near = along_line(part, lambda layer: layer ^ 1)
    second = along_line(part, lambda layer: 3 - layer)
    beside = column_swap(part)
    block_swapped = core_swap(embeddings)
    own, far, other = [part], [beside], [half(embeddings, 1 - member)]
    (own_sums,) = add_sums([embeddings, block_swapped], (None, own, 0, 2))

    second, near, beside, own_sums = stage((second, near, beside, own_sums))
    third = along_line(jnp.where(inner, second, part), {0: 2, 1: 0, 2: 3, 3: 1}.get)
    near_beside = column_swap(near)
    (second_over,) = over_members(second)
    near_swapped, second_swapped = core_swap(near), core_swap(second)
    far = [beside]
    far_sums, other_sums, own_sums = add_sums(
        [embeddings, block_swapped, second, second_swapped, near, near_swapped],
        (None, far, 0, 4),
        (None, other, 4, 6),
        (own_sums, own, 4, 6),
    )

    own_sums, far_sums, other_sums, third = stage((own_sums, far_sums, other_sums, third))
    first_half, second_half = third[: share // 2], third[share // 2 :]
    (third_over,) = over_members(first_half)
    third_beside = column_swap(second_half)
    third_swapped = core_swap_parts(third, 1)
    near_beside_swapped, second_over_swapped = core_swap_parts(near_beside, 1), core_swap_parts(second_over, 1)
    other_sums, far_sums = add_sums(
        [
            near_beside,
            near_beside_swapped,
            second_half,
            third_swapped[share // 2 :],
            first_half,
            third_swapped[: share // 2],
            second_over,
            second_over_swapped,
        ],
        (other_sums, other, 0, 4),
        (far_sums, far, 4, 8),
    )

    own_sums, far_sums, other_sums, third_beside, third_over = stage(
        (own_sums, far_sums, other_sums, third_beside, third_over)
    )
    third_over_swapped, third_beside_swapped = core_swap(third_over), core_swap(third_beside)
    far_sums, other_sums = add_sums([third_over, third_beside], (far_sums, far, 0, 1), (other_sums, other, 1, 2))
    far_sums, other_sums = add_sums(
        [third_over_swapped, third_beside_swapped], (far_sums, far, 0, 1), (other_sums, other, 1, 2)
    )
    own_sums, other_sums, far_sums = stage((own_sums, other_sums, far_sums))
    far_returned = column_swap(far_sums[0])
    (other_returned,) = over_members(other_sums[0])
    rest = [second, second_swapped, near_beside, near_beside_swapped, second_over, second_over_swapped, third, third_swapped, third_over, third_over_swapped, third_beside, third_beside_swapped]
    (own_sums,) = add_sums(rest, (own_sums, own, 0, len(rest)))
    return (own_sums[0] + far_returned + other_returned) * math.exp(-2.0)


def local(embeddings):
    layers = lax.axis_size("team") // (CORES * COLUMNS)
    return (staged if layers == 4 and lax.axis_size("member") == 2 else plain)(embeddings)


def solution(mesh):
    return jax.shard_map(
        local,
        mesh=mesh,
        in_specs=(P("team", None),),
        out_specs=P(("team", "member"), None),
        check_vma=False,
    )
```
